32 devices in a mesh: row: 4 (over y, x), col: 8 (over z, core).
Axes of the slice: x: 2, y: 2, z: 4, core: 2. Of those that a mesh axis runs over, the one named last changes fastest.
Arguments:
- pair_state: bfloat16 [1536, 1536, 128], P('row', 'col'), may hold values from -6 to 6
- single_state: bfloat16 [1536, 384], P(('row', 'col')), may hold values from -6 to 6
- token_mask: int32 [1536], P('col'), may hold values 0 or 1
- first_gate: bfloat16 [128, 512], replicated, may hold values from -0.5 to 0.5
- first_up: bfloat16 [128, 512], replicated, may hold values from -0.5 to 0.5
- first_down: bfloat16 [512, 128], replicated, may hold values from -0.25 to 0.25
- bias_weight: bfloat16 [128, 16], replicated, may hold values from -21 to 21
- query_weight: bfloat16 [384, 384], replicated, may hold values from -0.3125 to 0.3125
- key_weight: bfloat16 [384, 384], replicated, may hold values from -0.3125 to 0.3125
- value_weight: bfloat16 [384, 384], replicated, may hold values from -0.3125 to 0.3125
- gate_weight: bfloat16 [384, 384], replicated, may hold values from -0.3125 to 0.3125
- out_weight: bfloat16 [384, 384], replicated, may hold values from -0.3125 to 0.3125
- second_gate: bfloat16 [128, 512], replicated, may hold values from -0.5 to 0.5
- second_up: bfloat16 [128, 512], replicated, may hold values from -0.5 to 0.5
- second_down: bfloat16 [512, 128], replicated, may hold values from -0.25 to 0.25
Outputs:
- pair_out: bfloat16 [1536, 1536, 128], P('row', 'col')
- single_out: bfloat16 [1536, 384], P('row')
The draws below stay inside these ranges and needn't reach their ends.
All inputs are finite; a program needn't handle non-finite values. No bound on the sum of `token_mask` on one device may be relied on, other than what follows from the above.
Results may differ from the reference program's by a relative error of at most 0.011.
Values may be sent and summed in bfloat16 or wider, within the bound.
A program may use at most 384 MiB of HBM per device.

```python
import math
import jax
import jax.numpy as jnp
from jax import lax

C = 128
HID = 512
S = 384
HEADS = 16
HEAD_DIM = 24
N = 1536


def draw_bias_weight(key, part):
    first_key = jax.random.fold_in(key, 11)
    second_key = jax.random.fold_in(key, 12)
    entries = jax.random.normal(first_key, (C, HEADS), jnp.float32)
    scales = jnp.exp(jax.random.uniform(second_key, (HEADS,), jnp.float32, math.log(0.5), math.log(3.0)))
    return jnp.clip(entries * scales[None, :] / math.sqrt(C), -21.0, 21.0).astype(jnp.bfloat16)


def place_ends(values, stream_key, low, high):
    longest = values.shape.index(max(values.shape))
    spots = []
    for shift in (0, 1):
        where = [jax.random.randint(jax.random.fold_in(stream_key, axis), (), 0, length) for axis, length in enumerate(values.shape)]
        where[longest] = (where[longest] + shift) % values.shape[longest]
        spots.append(tuple(where))
    return values.at[spots[0]].set(low).at[spots[1]].set(high)


def level_of(stream_key, shape, shards, least, top_value):
    factor_of, own = 1.0, jax.random.fold_in(stream_key, 6)
    for position, blocks in shards:
        heights = jnp.exp(jax.random.uniform(jax.random.fold_in(own, position), (blocks,), jnp.float32, least / len(shards), top_value / len(shards)))
        factor_of = factor_of * jnp.repeat(heights, shape[position] // blocks).reshape([-1 if axis == position else 1 for axis in range(len(shape))])
    return factor_of


def scatter_about(key, dims, deviation, most, split=(), held_as=jnp.bfloat16):
    factor_of = level_of(key, dims, split, -0.22, 0.18) if split else 1.0
    drawn = jax.random.normal(key, dims, jnp.float32) * deviation * factor_of
    return jnp.minimum(jnp.maximum(drawn, -most), most).astype(held_as)


def setup_inputs(seed: int = 0) -> dict:
    streams_of = jax.random.split(jax.random.key(seed), 16)
    return {
        "pair_state": scatter_about(streams_of[0], (N, N, C), 1.0, 6.0, ((0, 4), (1, 8))),
        "single_state": scatter_about(streams_of[1], (N, S), 1.0, 6.0, ((0, 32),)),
        "token_mask": place_ends((jax.random.randint(streams_of[2], (N,), 0, 4) < 3).astype(jnp.int32), jax.random.fold_in(streams_of[2], 1), 0, 1),
        "first_gate": scatter_about(streams_of[3], (C, HID), C ** -0.5, 0.5),
        "first_up": scatter_about(streams_of[4], (C, HID), C ** -0.5, 0.5),
        "first_down": scatter_about(streams_of[5], (HID, C), HID ** -0.5, 0.25),
        "bias_weight": draw_bias_weight(jax.random.fold_in(streams_of[15], 71), 0),
        "query_weight": scatter_about(streams_of[7], (S, S), S ** -0.5, 0.3125),
        "key_weight": scatter_about(streams_of[8], (S, S), S ** -0.5, 0.3125),
        "value_weight": scatter_about(streams_of[9], (S, S), S ** -0.5, 0.3125),
        "gate_weight": scatter_about(streams_of[10], (S, S), S ** -0.5, 0.3125),
        "out_weight": scatter_about(streams_of[11], (S, S), S ** -0.5, 0.3125),
        "second_gate": scatter_about(streams_of[12], (C, HID), C ** -0.5, 0.5),
        "second_up": scatter_about(streams_of[13], (C, HID), C ** -0.5, 0.5),
        "second_down": scatter_about(streams_of[14], (HID, C), HID ** -0.5, 0.25),
    }


def norm_rows(values):
    centre = lax.optimization_barrier(jnp.mean(values, axis=-1, keepdims=True))
    centred = values - centre
    spread = lax.optimization_barrier(jnp.mean(centred * centred, axis=-1, keepdims=True))
    return centred * lax.rsqrt(spread + 1e-05)

def transition(widened, w_gate, w_up, w_down):
    layout = widened.shape
    flat_cells = widened.reshape(-1, layout[-1])
    normed = norm_rows(flat_cells).astype(jnp.bfloat16)
    gate_act = jnp.dot(normed, w_gate, preferred_element_type=jnp.float32)
    up_act = jnp.dot(normed, w_up, preferred_element_type=jnp.float32)
    hidden = (jax.nn.silu(gate_act) * up_act).astype(jnp.bfloat16)
    return jnp.dot(hidden, w_down, preferred_element_type=jnp.float32).reshape(layout)

def reference(pair_state, single_state, token_mask, first_gate, first_up, first_down, bias_weight, query_weight, key_weight, value_weight, gate_weight, out_weight, second_gate, second_up, second_down):
    blocks = N // 32
    stacked = pair_state.reshape(blocks, 32, N, C)

    def first_pass(pair_block):
        widened = pair_block.astype(jnp.float32)
        updated = (widened + transition(widened, first_gate, first_up, first_down)).astype(jnp.bfloat16)
        normed = norm_rows(updated.astype(jnp.float32)).astype(jnp.bfloat16)
        pair_bias = jnp.einsum('ijc,ch->ijh', normed.astype(jnp.float32), bias_weight.astype(jnp.float32), precision=lax.Precision.HIGHEST)
        return (updated, pair_bias)
    updated, pair_bias = lax.map(first_pass, stacked)
    updated = updated.reshape(N, N, C)
    pair_bias = jnp.transpose(pair_bias.reshape(N, N, HEADS), (2, 0, 1))
    flipped = jnp.transpose(updated, (1, 0, 2))

    def second_pass(halves):
        summed = halves[0].astype(jnp.float32) + halves[1].astype(jnp.float32)
        return (summed + transition(summed, second_gate, second_up, second_down)).astype(jnp.bfloat16)
    pair_out = lax.map(second_pass, (updated.reshape(blocks, 32, N, C), flipped.reshape(blocks, 32, N, C))).reshape(N, N, C)
    single_normed = norm_rows(single_state.astype(jnp.float32)).astype(jnp.bfloat16)
    queries = jnp.dot(single_normed, query_weight, preferred_element_type=jnp.float32).astype(jnp.bfloat16)
    key_vecs = jnp.dot(single_normed, key_weight, preferred_element_type=jnp.float32).astype(jnp.bfloat16)
    value_vecs = jnp.dot(single_normed, value_weight, preferred_element_type=jnp.float32).astype(jnp.bfloat16)
    gate_act = jax.nn.sigmoid(jnp.dot(single_normed, gate_weight, preferred_element_type=jnp.float32))
    query_heads = queries.astype(jnp.float32).reshape(N, HEADS, HEAD_DIM)
    key_heads = key_vecs.astype(jnp.float32).reshape(N, HEADS, HEAD_DIM)
    value_heads = value_vecs.astype(jnp.float32).reshape(N, HEADS, HEAD_DIM)
    scores = jnp.einsum('ihd,jhd->hij', query_heads, key_heads, precision=lax.Precision.HIGHEST) * (1.0 / math.sqrt(HEAD_DIM)) + pair_bias
    scores = jnp.where(token_mask[None, None, :] > 0, scores, -1000000000.0)
    row_top = lax.optimization_barrier(jnp.max(scores, axis=2, keepdims=True))
    weights = jnp.exp(scores - row_top)
    numerator = jnp.einsum('hij,jhd->ihd', weights, value_heads, precision=lax.Precision.HIGHEST)
    denominator = jnp.transpose(lax.optimization_barrier(jnp.sum(weights, axis=2)), (1, 0))
    attended = (numerator / denominator[:, :, None]).reshape(N, S)
    gated = (gate_act * attended).astype(jnp.bfloat16)
    single_out = (single_state.astype(jnp.float32) + jnp.dot(gated, out_weight, preferred_element_type=jnp.float32)).astype(jnp.bfloat16)
    return (pair_out, single_out)
```

```python
import functools
import math

import jax
import jax.numpy as jnp
from jax import lax
from jax.experimental import pallas as pl
from jax.experimental.pallas import tpu as pltpu
from jax.sharding import PartitionSpec as P

VMEM_LIMIT = 56 * 1024 * 1024


def norm_rows(values):
    centre = jnp.mean(values, axis=-1, keepdims=True)
    centred = values - centre
    spread = jnp.mean(centred * centred, axis=-1, keepdims=True)
    return centred * lax.rsqrt(spread + 1e-05)


def transition(cells, w_in, w_down):
    normed = norm_rows(cells).astype(jnp.bfloat16)
    both = jnp.dot(normed, w_in, preferred_element_type=jnp.float32)
    hid = both.shape[1] // 2
    half_gate = both[:, :hid]
    hidden = (half_gate * (1.0 + jnp.tanh(half_gate)) * both[:, hid:]).astype(jnp.bfloat16)
    return cells + jnp.dot(hidden, w_down, preferred_element_type=jnp.float32)


def first_kernel(pair_ref, w_in_ref, w_down_ref, bias_w_ref, updated_ref, bias_ref):
    rows, cols, channels = pair_ref.shape
    cells = pair_ref[...].reshape(rows * cols, channels).astype(jnp.float32)
    updated = transition(cells, w_in_ref[...], w_down_ref[...]).astype(jnp.bfloat16)
    updated_ref[...] = updated.reshape(rows, cols, channels)
    normed = norm_rows(updated.astype(jnp.float32)).astype(jnp.bfloat16)
    bias_ref[...] = lax.dot_general(
        bias_w_ref[...], normed, (((1,), (1,)), ((), ())), preferred_element_type=jnp.float32
    )


def first_pass(pair_state, w_in, w_down, bias_t):
    rows, cols, channels = pair_state.shape
    heads = bias_t.shape[0]
    step = math.gcd(rows, 8)
    whole = lambda a: pl.BlockSpec(a.shape, lambda i: (0, 0))
    return pl.pallas_call(
        first_kernel,
        grid=(rows // step,),
        in_specs=[
            pl.BlockSpec((step, cols, channels), lambda i: (i, 0, 0)),
            whole(w_in),
            whole(w_down),
            whole(bias_t),
        ],
        out_specs=[
            pl.BlockSpec((step, cols, channels), lambda i: (i, 0, 0)),
            pl.BlockSpec((heads, step * cols), lambda i: (0, i)),
        ],
        out_shape=[
            jax.ShapeDtypeStruct(pair_state.shape, jnp.bfloat16),
            jax.ShapeDtypeStruct((heads, rows * cols), jnp.float32),
        ],
        compiler_params=pltpu.CompilerParams(vmem_limit_bytes=VMEM_LIMIT),
    )(pair_state, w_in, w_down, bias_t)


def second_kernel(updated_ref, arrived_ref, w_in_ref, w_down_ref, out_ref):
    rows, cols, channels = updated_ref.shape
    flipped = jnp.swapaxes(arrived_ref[0].astype(jnp.float32), 0, 1)
    summed = updated_ref[...].astype(jnp.float32) + flipped
    part = rows // 2
    for start in range(0, rows, part):
        cells = summed[start : start + part].reshape(part * cols, channels)
        made = transition(cells, w_in_ref[...], w_down_ref[...]).astype(jnp.bfloat16)
        out_ref[start : start + part] = made.reshape(part, cols, channels)


def second_pass(updated, arrived, w_in, w_down):
    rows, cols, channels = updated.shape
    sources = arrived.shape[0]
    span = rows // sources
    step = math.gcd(span, 16)
    blocks = span // step
    whole = lambda a: pl.BlockSpec(a.shape, lambda s, i: (0, 0))
    own = pl.BlockSpec((step, cols, channels), lambda s, i: (s * blocks + i, 0, 0))
    return pl.pallas_call(
        second_kernel,
        grid=(sources, blocks),
        in_specs=[
            own,
            pl.BlockSpec((1, cols, step, channels), lambda s, i: (s, 0, i, 0)),
            whole(w_in),
            whole(w_down),
        ],
        out_specs=own,
        out_shape=jax.ShapeDtypeStruct(updated.shape, jnp.bfloat16),
        compiler_params=pltpu.CompilerParams(vmem_limit_bytes=VMEM_LIMIT),
    )(updated, arrived, w_in, w_down)


MESH = pl.DeviceIdType.MESH


class Exchange:
    def __init__(self, row_count, col_count, chunks, own, first, second, last, sems):
        self.row_count, self.col_count = row_count, col_count
        self.rep = col_count // row_count
        self.own, self.first, self.second, self.last = own, first, second, last
        self.sems = sems
        self.size = own.shape[2] // chunks
        self.row, self.col = lax.axis_index("row"), lax.axis_index("col")

    def rows(self, chunk):
        return pl.ds(chunk * self.size, self.size)

    def hop(self, number, chunk, offset, local=False):
        rows = self.rows(chunk)
        row, col, rep = self.row, self.col, self.rep
        if number == 1:
            to = lax.rem(row + offset, self.row_count)
            source, target = self.own.at[:, to, rows], self.first.at[row, :, rows]
            device = (to, col)
        elif number == 2:
            to = lax.rem(col + offset, self.col_count)
            source = self.first.at[to // rep, lax.rem(to, rep), rows]
            target = self.second.at[col, rows]
            device = (row, to)
        else:
            to = lax.rem(row + offset, self.row_count)
            source = self.second.at[pl.ds(to * rep, rep), rows]
            target = self.last.at[:, row, rows]
            device = (to, col)
        send, recv = self.sems[2 * number - 2], self.sems[2 * number - 1]
        if local:
            return pltpu.make_async_copy(source, target, recv.at[chunk, 0])
        return pltpu.make_async_remote_copy(
            src_ref=source,
            dst_ref=target,
            send_sem=send.at[chunk, offset],
            recv_sem=recv.at[chunk, offset],
            device_id=device,
            device_id_type=MESH,
        )

    def count(self, number):
        return self.col_count if number == 2 else self.row_count

    def each(self, number, act):
        def step(offset, carry):
            act(offset)
            return carry

        lax.fori_loop(1, self.count(number), step, 0)

    def start(self, number, chunk):
        self.each(number, lambda o: self.hop(number, chunk, o).start())
        self.hop(number, chunk, 0, True).start()

    def arrive(self, number, chunk):
        self.each(number, lambda o: self.hop(number, chunk, o).wait_recv())
        self.hop(number, chunk, 0, True).wait()

    def finish(self, number, chunk):
        self.each(number, lambda o: self.hop(number, chunk, o).wait_send())

    def greet(self):
        barrier = pltpu.get_barrier_semaphore()

        def in_col(offset):
            to = lax.rem(self.row + offset, self.row_count)
            pl.semaphore_signal(barrier, inc=1, device_id=(to, self.col), device_id_type=MESH)

        def in_row(offset):
            to = lax.rem(self.col + offset, self.col_count)
            pl.semaphore_signal(barrier, inc=1, device_id=(self.row, to), device_id_type=MESH)

        self.each(1, in_col)
        self.each(2, in_row)
        pl.semaphore_wait(barrier, self.row_count + self.col_count - 2)


def exchange_kernel(row_count, col_count, chunks, own, first, second, last, *sems):
    trip = Exchange(row_count, col_count, chunks, own, first, second, last, sems)
    trip.greet()
    for step in range(chunks + 2):
        if step < chunks:
            trip.start(1, step)
        if 1 <= step <= chunks:
            trip.arrive(1, step - 1)
            trip.start(2, step - 1)
        if step >= 2:
            trip.arrive(2, step - 2)
            trip.start(3, step - 2)
    for chunk in range(chunks):
        trip.arrive(3, chunk)
        for number in (1, 2, 3):
            trip.finish(number, chunk)


def mirror(updated):
    rows, cols, channels = updated.shape
    row_count, col_count = lax.axis_size("row"), lax.axis_size("col")
    rep = col_count // row_count
    part = rows // rep // row_count
    chunks = math.gcd(part, 6)
    sems = []
    for count in (row_count, col_count, row_count):
        sems += [pltpu.SemaphoreType.DMA((chunks, count))] * 2
    shape = lambda *lead: jax.ShapeDtypeStruct((*lead, part, cols, channels), jnp.bfloat16)
    outs = pl.pallas_call(
        functools.partial(exchange_kernel, row_count, col_count, chunks),
        in_specs=[pl.BlockSpec(memory_space=pl.ANY)],
        out_specs=[pl.BlockSpec(memory_space=pl.ANY)] * 3,
        out_shape=[shape(row_count, rep), shape(col_count), shape(rep, row_count)],
        scratch_shapes=sems,
        compiler_params=pltpu.CompilerParams(
            collective_id=0, has_side_effects=True, vmem_limit_bytes=VMEM_LIMIT
        ),
    )(updated.reshape(rep, row_count, part, cols, channels))
    return outs[2].reshape(rep, cols, cols, channels)


def spread_2(value, axis, source):
    kept = jnp.where(lax.axis_index(axis) == source, value, 0).astype(value.dtype)
    return lax.psum(kept, axis)


def project_keys(key_rows, key_weight, value_weight):
    normed = norm_rows(key_rows.astype(jnp.float32)).astype(jnp.bfloat16)
    key_vecs = jnp.dot(normed, key_weight, preferred_element_type=jnp.float32).astype(jnp.bfloat16)
    value_vecs = jnp.dot(normed, value_weight, preferred_element_type=jnp.float32).astype(
        jnp.bfloat16
    )
    return (key_vecs, value_vecs)


def combined(numerator, total, top, axis):
    width, heads = numerator.shape[1], top.shape[1]
    parts = lax.all_gather(jnp.concatenate([numerator, total, top], axis=1), axis)
    tops = parts[:, :, width + heads :]
    scale = jnp.exp(tops - jnp.max(tops, axis=0))
    wide = jnp.repeat(scale, width // heads, axis=2)
    return (
        jnp.sum(parts[:, :, :width] * wide, axis=0),
        jnp.sum(parts[:, :, width : width + heads] * scale, axis=0),
    )


def body(
    pair_state,
    single_state,
    token_mask,
    first_gate,
    first_up,
    first_down,
    bias_weight,
    query_weight,
    key_weight,
    value_weight,
    gate_weight,
    out_weight,
    second_gate,
    second_up,
    second_down,
):
    rows_here, keys_here, channels = pair_state.shape
    col_index = lax.axis_index("col")
    first_in = jnp.concatenate([first_gate * 0.5, first_up], axis=1)
    second_in = jnp.concatenate([second_gate * 0.5, second_up], axis=1)
    updated, flat_bias = first_pass(pair_state, first_in, first_down, bias_weight.T)
    arrived = mirror(updated)
    query_rows = lax.all_gather(single_state, "col", axis=0, tiled=True)
    query_normed = norm_rows(query_rows.astype(jnp.float32)).astype(jnp.bfloat16)
    queries = jnp.dot(query_normed, query_weight, preferred_element_type=jnp.float32).astype(
        jnp.bfloat16
    )
    gate_act = jax.nn.sigmoid(
        jnp.dot(query_normed, gate_weight, preferred_element_type=jnp.float32)
    )
    rep = rows_here // keys_here
    own_rows = lax.dynamic_slice_in_dim(query_rows, col_index % rep * keys_here, keys_here, 0)
    own_keys, own_values = project_keys(own_rows, key_weight, value_weight)
    both_vecs = spread_2(jnp.stack([own_keys, own_values]), "row", col_index // rep)
    key_vecs, value_vecs = both_vecs[0], both_vecs[1]
    head_count = bias_weight.shape[1]
    head_dim = queries.shape[1] // head_count
    pair_bias = flat_bias.reshape(head_count, rows_here, keys_here)
    scores = (
        jnp.einsum(
            "ihd,jhd->hij",
            queries.reshape(rows_here, head_count, head_dim),
            key_vecs.reshape(keys_here, head_count, head_dim),
            preferred_element_type=jnp.float32,
        )
        * (1.0 / math.sqrt(head_dim))
        + pair_bias
    )
    scores = jnp.where(token_mask[None, None, :] > 0, scores, -1000000000.0)
    value_heads = value_vecs.astype(jnp.float32).reshape(keys_here, head_count, head_dim)
    local_top = jnp.max(scores, axis=2)
    weights = jnp.exp(scores - local_top[:, :, None])
    numerator = jnp.einsum(
        "hij,jhd->ihd", weights, value_heads, precision=lax.Precision.HIGHEST
    ).reshape(rows_here, -1)
    numerator, total = combined(numerator, jnp.sum(weights, axis=2).T, local_top.T, "col")
    attended = (
        numerator.reshape(rows_here, head_count, head_dim) / total[:, :, None]
    ).reshape(rows_here, -1)
    gated = (gate_act * attended).astype(jnp.bfloat16)
    single_out = (
        query_rows.astype(jnp.float32)
        + jnp.dot(gated, out_weight, preferred_element_type=jnp.float32)
    ).astype(jnp.bfloat16)
    pair_out = second_pass(updated, arrived, second_in, second_down)
    return (pair_out, single_out)


def solution(mesh):
    in_specs = (P("row", "col", None), P(("row", "col"), None), P("col")) + (P(),) * 12
    out_specs = (P("row", "col", None), P("row", None))
    return jax.shard_map(body, mesh=mesh, in_specs=in_specs, out_specs=out_specs, check_vma=False)
```
